32 devices in a mesh: dp: 8 (over z, y), ctx: 4 (over x, core).
Axes of the slice: x: 2, y: 2, z: 4, core: 2. Of those that a mesh axis runs over, the one named last changes fastest.
Arguments:
- tokens: bfloat16 [8, 1024, 768], P('dp', 'ctx'), may hold values from -6 to 6
- segments: int32 [8, 1024], P('dp', 'ctx'), may hold values from 0 to 2, as said below
- ln1_gain: bfloat16 [2, 768], P(None, ('dp', 'ctx')), may hold values from 0.5 to 1.5
- ln1_bias: bfloat16 [2, 768], P(None, ('dp', 'ctx')), may hold values from -1.75 to 1.75
- w_query: bfloat16 [2, 768, 768], P(None, ('dp', 'ctx')), may hold values from -0.21875 to 0.21875
- b_query: bfloat16 [2, 768], P(None, ('dp', 'ctx')), may hold values from -3 to 3
- w_key: bfloat16 [2, 768, 768], P(None, ('dp', 'ctx')), may hold values from -0.21875 to 0.21875
- w_value: bfloat16 [2, 768, 768], P(None, ('dp', 'ctx')), may hold values from -0.21875 to 0.21875
- b_value: bfloat16 [2, 768], P(None, ('dp', 'ctx')), may hold values from -0.3125 to 0.3125
- w_out: bfloat16 [2, 768, 768], P(None, ('dp', 'ctx')), may hold values from -1.75 to 1.75
- b_out: bfloat16 [2, 768], P(None, ('dp', 'ctx')), may hold values from -1.75 to 1.75
- ln2_gain: bfloat16 [2, 768], P(None, ('dp', 'ctx')), may hold values from 0.5 to 1.5
- ln2_bias: bfloat16 [2, 768], P(None, ('dp', 'ctx')), may hold values from -1.75 to 1.75
- w_up: bfloat16 [2, 768, 3072], P(None, ('dp', 'ctx')), may hold values from -0.21875 to 0.21875
- b_up: bfloat16 [2, 3072], P(None, ('dp', 'ctx')), may hold values from -3 to 3
- w_down: bfloat16 [2, 3072, 768], P(None, ('dp', 'ctx')), may hold values from -0.109375 to 0.109375
- b_down: bfloat16 [2, 768], P(None, ('dp', 'ctx')), may hold values from -1.75 to 1.75
- out_grad: bfloat16 [8, 1024, 768], P('dp', 'ctx'), may hold values from -6 to 6
Outputs:
- output: bfloat16 [8, 1024, 768], P('dp', 'ctx')
- input_grad: float32 [8, 1024, 768], P('dp', 'ctx')
- grad_ln1_gain: float32 [2, 768], P(None, ('dp', 'ctx'))
- grad_ln1_bias: float32 [2, 768], P(None, ('dp', 'ctx'))
- grad_w_query: float32 [2, 768, 768], P(None, ('dp', 'ctx'))
- grad_b_query: float32 [2, 768], P(None, ('dp', 'ctx'))
- grad_w_key: float32 [2, 768, 768], P(None, ('dp', 'ctx'))
- grad_w_value: float32 [2, 768, 768], P(None, ('dp', 'ctx'))
- grad_b_value: float32 [2, 768], P(None, ('dp', 'ctx'))
- grad_w_out: float32 [2, 768, 768], P(None, ('dp', 'ctx'))
- grad_b_out: float32 [2, 768], P(None, ('dp', 'ctx'))
- grad_ln2_gain: float32 [2, 768], P(None, ('dp', 'ctx'))
- grad_ln2_bias: float32 [2, 768], P(None, ('dp', 'ctx'))
- grad_w_up: float32 [2, 768, 3072], P(None, ('dp', 'ctx'))
- grad_b_up: float32 [2, 3072], P(None, ('dp', 'ctx'))
- grad_w_down: float32 [2, 3072, 768], P(None, ('dp', 'ctx'))
- grad_b_down: float32 [2, 768], P(None, ('dp', 'ctx'))
The draws below stay inside these ranges and needn't reach their ends.
Inputs may be any that keep to these rules, and one draw needn't show every extreme that they name: `segments`: in each sequence the document numbers never fall. Document 1 begins after position 0 and within the first 256 positions, and ends within the last 256 positions; document 0 is never empty, document 2 may be.
All inputs are finite; a program needn't handle non-finite values.
Results may differ from the reference program's by a relative error of at most 0.025.
Values may be sent and summed in bfloat16 or wider, within the bound.
A program may use at most 320 MiB of HBM per device.

```python
import jax
import jax.numpy as jnp
from jax import lax

D = 768
FF = 3072
H = 12
HD = 64
LAYERS = 2
SEQ = 1024
TOK_DEV = 256
ROWS = 8


def draw_segments(key, part):
    key = jax.random.fold_in(key, 11)
    first_key, last_key = jax.random.split(key)
    begin = jax.random.randint(first_key, (ROWS, 1), 1, TOK_DEV)
    finish = jax.random.randint(last_key, (ROWS, 1), SEQ - TOK_DEV + 1, SEQ + 1)
    places = jnp.arange(SEQ)[None, :]
    return (places >= begin).astype(jnp.int32) + (places >= finish).astype(jnp.int32)


def shard_levels(own_key, dims, shards, smallest, largest):
    def one(axis_at, blocks):
        steps = jax.random.uniform(jax.random.fold_in(jax.random.fold_in(own_key, 6), axis_at), (blocks,), jnp.float32, smallest / len(shards), largest / len(shards))
        return jnp.repeat(jnp.exp(steps), dims[axis_at] // blocks).reshape((-1,) + (1,) * (len(dims) - axis_at - 1))

    loudness = one(*shards[0])
    for cut in shards[1:]:
        loudness = loudness * one(*cut)
    return loudness


def bell_draw(stream_key, dims, scale, bound, pieces=(), held_as=jnp.bfloat16):
    entries = scale * jax.random.normal(stream_key, dims, jnp.float32)
    if pieces:
        entries = entries * shard_levels(stream_key, dims, pieces, -0.22, 0.18)
    return jnp.clip(entries, -bound, bound).astype(held_as)


def setup_inputs(seed: int = 0) -> dict:
    key_list = jax.random.split(jax.random.key(seed), 19)
    tokens = bell_draw(key_list[0], (ROWS, SEQ, D), 1.0, 6.0, ((0, 8), (1, 4)))
    segments = draw_segments(jax.random.fold_in(key_list[18], 71), 0)
    ln1_gain = jnp.clip(1.0 + 0.1 * jax.random.normal(key_list[2], (LAYERS, D), jnp.float32), 0.5, 1.5).astype(jnp.bfloat16)
    ln1_bias = bell_draw(key_list[3], (LAYERS, D), 0.3, 1.75, ((1, 32),))
    w_query = bell_draw(key_list[4], (LAYERS, D, D), D ** -0.5, 0.21875, ((1, 32),))
    b_query = bell_draw(key_list[5], (LAYERS, D), 0.5, 3.0, ((1, 32),))
    w_key = bell_draw(key_list[6], (LAYERS, D, D), D ** -0.5, 0.21875, ((1, 32),))
    w_value = bell_draw(key_list[7], (LAYERS, D, D), D ** -0.5, 0.21875, ((1, 32),))
    b_value = bell_draw(key_list[8], (LAYERS, D), 0.05, 0.3125, ((1, 32),))
    w_out = bell_draw(key_list[9], (LAYERS, D, D), (D // 64) ** -0.5, 1.75, ((1, 32),))
    b_out = bell_draw(key_list[10], (LAYERS, D), 0.3, 1.75, ((1, 32),))
    ln2_gain = jnp.clip(1.0 + 0.1 * jax.random.normal(key_list[11], (LAYERS, D), jnp.float32), 0.5, 1.5).astype(jnp.bfloat16)
    ln2_bias = bell_draw(key_list[12], (LAYERS, D), 0.3, 1.75, ((1, 32),))
    w_up = bell_draw(key_list[13], (LAYERS, D, FF), D ** -0.5, 0.21875, ((1, 32),))
    b_up = bell_draw(key_list[14], (LAYERS, FF), 0.5, 3.0, ((1, 32),))
    w_down = bell_draw(key_list[15], (LAYERS, FF, D), FF ** -0.5, 0.109375, ((1, 32),))
    b_down = bell_draw(key_list[16], (LAYERS, D), 0.3, 1.75, ((1, 32),))
    out_grad = bell_draw(key_list[17], (ROWS, SEQ, D), 1.0, 6.0, ((0, 8), (1, 4)))
    return {"tokens": tokens, "segments": segments, "ln1_gain": ln1_gain, "ln1_bias": ln1_bias, "w_query": w_query, "b_query": b_query, "w_key": w_key, "w_value": w_value, "b_value": b_value, "w_out": w_out, "b_out": b_out, "ln2_gain": ln2_gain, "ln2_bias": ln2_bias, "w_up": w_up, "b_up": b_up, "w_down": w_down, "b_down": b_down, "out_grad": out_grad}


EPSILON = 1e-05
MASKED = -1e+30

@jax.custom_vjp
def low(v):
    return lax.optimization_barrier(v.astype(jnp.bfloat16)).astype(jnp.float32)

@jax.custom_vjp
def low_back(v):
    return v

def low_keep(v):
    return (low(v), None)

def low_pass(kept, grad):
    return (grad,)

def back_keep(v):
    return (v, None)

def back_low(kept, grad):
    return (low(grad),)
low.defvjp(low_keep, low_pass)
low_back.defvjp(back_keep, back_low)

def both_ways(values):
    return low_back(low(values))

def product(left_op, right_op):
    return jnp.dot(left_op, right_op, precision=lax.Precision.HIGHEST)

def layer_norm(values, gain_vec, shift_vec):
    centre = lax.optimization_barrier(jnp.mean(values, axis=-1, keepdims=True))
    centred = values - centre
    spread = lax.optimization_barrier(jnp.mean(centred * centred, axis=-1, keepdims=True))
    return centred * lax.rsqrt(spread + EPSILON) * gain_vec + shift_vec

def attention(queries, key_rows, values, seg_row):
    length = queries.shape[0]
    q_heads = queries.reshape(length, H, HD)
    k_heads = key_rows.reshape(length, H, HD)
    v_heads = values.reshape(length, H, HD)
    scores = jnp.einsum('qhd,khd->hqk', q_heads, k_heads, precision=lax.Precision.HIGHEST) * HD ** (-0.5)
    scores = low_back(scores)
    places = jnp.arange(length)
    allowed = (places[None, :] <= places[:, None]) & (seg_row[None, :] == seg_row[:, None])
    scores = jnp.where(allowed[None], scores, MASKED)
    highest = lax.optimization_barrier(jnp.max(scores, axis=-1, keepdims=True))
    weights = jnp.exp(scores - highest)
    probs_all = low(weights / lax.optimization_barrier(jnp.sum(weights, axis=-1, keepdims=True)))
    mixed_out = jnp.einsum('hqk,khd->qhd', probs_all, v_heads, precision=lax.Precision.HIGHEST)
    return mixed_out.reshape(length, H * HD)

def decoder_layer(stream, seg_row, params):
    gain_one, shift_one, w_query, b_query, w_key, w_value, b_value, w_out, b_out, gain_two, shift_two, w_up, b_up, w_down, b_down = params
    normed = low(layer_norm(stream, gain_one, shift_one))
    queries = both_ways(product(normed, w_query) + b_query)
    key_rows = both_ways(product(normed, w_key))
    values = both_ways(product(normed, w_value) + b_value)
    mixed_out = both_ways(attention(queries, key_rows, values, seg_row))
    stream = stream + low_back(product(mixed_out, w_out) + b_out)
    normed_two = low(layer_norm(stream, gain_two, shift_two))
    hidden = low_back(product(normed_two, w_up) + b_up)
    active = low(jax.nn.gelu(hidden, approximate=True))
    return stream + low_back(product(active, w_down) + b_down)

def reference(tokens, segments, ln1_gain, ln1_bias, w_query, b_query, w_key, w_value, b_value, w_out, b_out, ln2_gain, ln2_bias, w_up, b_up, w_down, b_down, out_grad):
    params = tuple((member.astype(jnp.float32) for member in (ln1_gain, ln1_bias, w_query, b_query, w_key, w_value, b_value, w_out, b_out, ln2_gain, ln2_bias, w_up, b_up, w_down, b_down)))

    def stacked(stream, seg_row, weights):
        for layer_no in range(LAYERS):
            stream = decoder_layer(stream, seg_row, tuple((member[layer_no] for member in weights)))
        return stream

    def one_row(totals, row_data):
        row_tokens, seg_row, row_grad = row_data
        result, pullback = jax.vjp(lambda stream, weights: stacked(stream, seg_row, weights), row_tokens.astype(jnp.float32), params)
        grad_in, grad_params = pullback(row_grad.astype(jnp.float32))
        totals = tuple((running + portion for running, portion in zip(totals, grad_params)))
        return (totals, (result.astype(jnp.bfloat16), grad_in))
    initial = tuple((jnp.zeros_like(member) for member in params))
    totals, (outputs, grads_in) = lax.scan(one_row, initial, (tokens, segments, out_grad))
    return (outputs, grads_in, totals[0], totals[1], totals[2], totals[3], totals[4], totals[5], totals[6], totals[7], totals[8], totals[9], totals[10], totals[11], totals[12], totals[13], totals[14])
```

```python
import jax
import jax.numpy as jnp
from jax import lax
from jax.sharding import PartitionSpec as P

H = 12
HD = 64


EPSILON = 1e-05
MASKED = -1e30


def matmul(left_op, right_op):
    return jnp.dot(left_op, right_op, preferred_element_type=jnp.float32)


def contract_rows(left_op, right_op):
    return lax.dot_general(
        left_op, right_op, (((0,), (0,)), ((), ())), preferred_element_type=jnp.float32
    )


def contract_cols(left_op, right_op):
    return lax.dot_general(
        left_op, right_op, (((1,), (1,)), ((), ())), preferred_element_type=jnp.float32
    )


def normalize(values):
    centre = jnp.mean(values, axis=-1, keepdims=True)
    centred = values - centre
    scale_vec = lax.rsqrt(jnp.mean(centred * centred, axis=-1, keepdims=True) + EPSILON)
    return (centred * scale_vec, scale_vec)


def norm_back(grad_in, normed, scale_vec, gain_vec):
    scaled = grad_in * gain_vec
    return scale_vec * (
        scaled
        - jnp.mean(scaled, axis=-1, keepdims=True)
        - normed * jnp.mean(scaled * normed, axis=-1, keepdims=True)
    )


def to_heads(blocks_in, parts):
    shards = lax.axis_size("ctx")
    row_count = blocks_in[0].shape[0]
    per = -(-H // shards)
    spare = (per * shards - H) * HD
    sent = jnp.stack([jnp.pad(b, ((0, 0), (0, spare))) for b in blocks_in])
    sent = sent.reshape(parts, row_count, shards, per * HD).transpose(2, 0, 1, 3)
    got = lax.all_to_all(sent, "ctx", 0, 0, tiled=True)
    got = got.reshape(shards, parts, row_count, per, HD).transpose(1, 3, 0, 2, 4)
    return got.reshape(parts, per, shards * row_count, HD)


def from_heads(heads_in):
    shards = lax.axis_size("ctx")
    parts, per, seq_len = heads_in.shape[:3]
    row_count = seq_len // shards
    sent = heads_in.reshape(parts, per, shards, row_count, HD).transpose(2, 0, 3, 1, 4)
    sent = sent.reshape(shards, parts, row_count, per * HD)
    got = lax.all_to_all(sent, "ctx", 0, 0, tiled=True)
    got = got.transpose(1, 2, 0, 3).reshape(parts, row_count, shards * per * HD)
    return got[:, :, : H * HD]


def head_dot(left_op, right_op, left_dim, right_dim):
    return lax.dot_general(
        left_op,
        right_op,
        (((left_dim,), (right_dim,)), ((0,), (0,))),
        preferred_element_type=jnp.float32,
    )


def attend_forward(heads, allowed):
    queries, key_rows, values = heads[0], heads[1], heads[2]
    scores = head_dot(queries, key_rows, 2, 2) * HD ** (-0.5)
    scores = jnp.where(allowed[None], scores, MASKED)
    highest = jnp.max(scores, axis=-1, keepdims=True)
    weights = jnp.exp(scores - highest)
    totals = jnp.sum(weights, axis=-1, keepdims=True)
    mixed_out = head_dot(weights.astype(jnp.bfloat16), values, 2, 1) / totals
    return (mixed_out, highest + jnp.log(totals))


def attend_back(heads, mixed_out, grad_mixed, log_total, allowed):
    queries, key_rows, values = heads[0], heads[1], heads[2]
    score_scale = HD ** (-0.5)
    row_delta = jnp.sum(grad_mixed.astype(jnp.float32) * mixed_out, axis=-1, keepdims=True)
    scores = head_dot(queries, key_rows, 2, 2) * score_scale
    probs = jnp.exp(jnp.where(allowed[None], scores, MASKED) - log_total)
    grad_p = head_dot(grad_mixed, values, 2, 2)
    grad_s = (probs * (grad_p - row_delta)).astype(jnp.bfloat16)
    grad_q = head_dot(grad_s, key_rows, 2, 1) * score_scale
    grad_k = head_dot(grad_s, queries, 1, 1) * score_scale
    grad_v = head_dot(probs.astype(jnp.bfloat16), grad_mixed, 1, 1)
    return jnp.stack([grad_q, grad_k, grad_v]).astype(jnp.bfloat16)


def layer_forward(stream, allowed, gathered):
    w_qkv, w_out, w_up, w_down, vectors = gathered
    gain_one, shift_one, b_query, b_value, b_out, gain_two, shift_two, b_down, b_up = vectors
    width = w_out.shape[1]
    normed_one, scale_one = normalize(stream)
    inputs_one = (normed_one * gain_one + shift_one).astype(jnp.bfloat16)
    bias_all = jnp.concatenate([b_query, jnp.zeros_like(b_query), b_value])
    projected = (matmul(inputs_one, w_qkv) + bias_all).astype(jnp.bfloat16)
    heads = to_heads([projected[:, p * width : (p + 1) * width] for p in range(3)], 3)
    mixed_out, log_total = attend_forward(heads, allowed)
    mixed_low = from_heads(mixed_out.astype(jnp.bfloat16)[None])[0]
    stream_mid = stream + matmul(mixed_low, w_out) + b_out
    normed_two, scale_two = normalize(stream_mid)
    inputs_two = (normed_two * gain_two + shift_two).astype(jnp.bfloat16)
    hidden = matmul(inputs_two, w_up) + b_up
    active = jax.nn.gelu(hidden, approximate=True).astype(jnp.bfloat16)
    stream_out = stream_mid + matmul(active, w_down) + b_down
    saved_acts = (
        normed_one,
        scale_one,
        inputs_one,
        heads,
        mixed_out,
        log_total,
        mixed_low,
        normed_two,
        scale_two,
        inputs_two,
        hidden,
        active,
    )
    return (stream_out, saved_acts)


def column_sums(values):
    return jnp.sum(values, axis=0, dtype=jnp.float32)


def layer_back(grad_out, allowed, gathered, saved_acts):
    w_qkv, w_out, w_up, w_down, vectors = gathered
    gain_one, shift_one, b_query, b_value, b_out, gain_two, shift_two, b_down, b_up = vectors
    (
        normed_one,
        scale_one,
        inputs_one,
        heads,
        mixed_out,
        log_total,
        mixed_low,
        normed_two,
        scale_two,
        inputs_two,
        hidden,
        active,
    ) = saved_acts
    width = w_out.shape[1]
    grad_branch = grad_out.astype(jnp.bfloat16)
    g_b_down = column_sums(grad_branch)
    g_w_down = contract_rows(active, grad_branch)
    grad_active = contract_cols(grad_branch, w_down)
    gelu_value, gelu_pull = jax.vjp(
        lambda inner_val: jax.nn.gelu(inner_val, approximate=True), hidden
    )
    grad_hidden = gelu_pull(grad_active)[0].astype(jnp.bfloat16)
    g_b_up = column_sums(grad_hidden)
    g_w_up = contract_rows(inputs_two, grad_hidden)
    grad_in_two = contract_cols(grad_hidden, w_up)
    g_gain_two = jnp.sum(grad_in_two * normed_two, axis=0)
    g_shift_two = jnp.sum(grad_in_two, axis=0)
    grad_mid = grad_out + norm_back(grad_in_two, normed_two, scale_two, gain_two)
    grad_attn = grad_mid.astype(jnp.bfloat16)
    g_b_out = column_sums(grad_attn)
    g_w_out = contract_rows(mixed_low, grad_attn)
    grad_mixed = contract_cols(grad_attn, w_out).astype(jnp.bfloat16)
    grad_heads = attend_back(
        heads, mixed_out, to_heads([grad_mixed], 1)[0], log_total, allowed
    )
    back = from_heads(grad_heads)
    projected = jnp.concatenate([back[0], back[1], back[2]], axis=1)
    g_bias = column_sums(projected)
    g_proj = contract_rows(inputs_one, projected)
    grad_in_one = contract_cols(projected, w_qkv)
    g_gain_one = jnp.sum(grad_in_one * normed_one, axis=0)
    g_shift_one = jnp.sum(grad_in_one, axis=0)
    grad_stream = grad_mid + norm_back(grad_in_one, normed_one, scale_one, gain_one)
    g_vectors = (
        g_gain_one,
        g_shift_one,
        g_bias[:width],
        g_bias[2 * width :],
        g_b_out,
        g_gain_two,
        g_shift_two,
        g_b_down,
        g_b_up,
    )
    return (grad_stream, (g_proj, g_w_out, g_w_up, g_w_down, g_vectors))


def column_pieces(matrix, width):
    return [matrix[..., c : c + width] for c in range(0, matrix.shape[-1], width)]


def pad_rows(packed):
    rows = packed.shape[-2]
    return jnp.pad(packed, ((0, 0),) * (packed.ndim - 2) + ((0, -rows % 16), (0, 0)))


def pack_vectors(vectors, width):
    joined = jnp.concatenate(vectors, axis=-1)
    short = -joined.shape[-1] % width
    joined = jnp.pad(joined, ((0, 0),) * (joined.ndim - 1) + ((0, short),))
    return joined.reshape(joined.shape[:-1] + (-1, width))


def gather_layer(matrices, vectors):
    w_query, w_key, w_value, w_out, w_up, w_down = matrices
    rows, width = w_query.shape
    up_count = w_up.shape[1] // width
    pieces = [w_query, w_key, w_value, w_out] + column_pieces(w_up, width)
    packed = jnp.concatenate(pieces + [w_down, pack_vectors(vectors, width)], axis=0)
    whole = lax.all_gather(pad_rows(packed), ("dp", "ctx"), axis=0, tiled=False)

    def taken(first, count):
        return whole[:, first : first + count].reshape(-1, width)

    parts = [taken(i * rows, rows) for i in range(4 + up_count)]
    start = (4 + up_count) * rows
    down = taken(start, w_down.shape[0])
    start += w_down.shape[0]
    flat = whole[:, start:].reshape(whole.shape[0], -1)
    out_vectors = []
    place = 0
    for vector in vectors:
        out_vectors.append(flat[:, place : place + vector.shape[0]].reshape(-1))
        place += vector.shape[0]
    return (
        jnp.concatenate(parts[:3], axis=1),
        parts[3],
        jnp.concatenate(parts[4:], axis=1),
        down,
        tuple(out_vectors),
    )


def scatter_layer(terms):
    g_proj, g_w_out, g_w_up, g_w_down, g_vectors = terms
    width = g_w_out.shape[1]
    shards = lax.axis_size(("dp", "ctx"))
    blocks = column_pieces(g_proj, width) + [g_w_out] + column_pieces(g_w_up, width) + [g_w_down]
    blocks = [b.astype(jnp.bfloat16).reshape(shards, -1, width) for b in blocks]
    rows, down_rows = blocks[0].shape[1], blocks[-1].shape[1]
    vectors = [v.astype(jnp.bfloat16).reshape(shards, -1) for v in g_vectors]
    packed = jnp.concatenate(blocks + [pack_vectors(vectors, width)], axis=1)
    own = lax.psum_scatter(
        pad_rows(packed), ("dp", "ctx"), scatter_dimension=0, tiled=False
    ).astype(jnp.float32)
    up_count = len(blocks) - 5
    parts = [own[i * rows : (i + 1) * rows] for i in range(4 + up_count)]
    start = (4 + up_count) * rows
    down = own[start : start + down_rows]
    flat = own[start + down_rows :].reshape(-1)
    out_vectors = []
    place = 0
    for vector in vectors:
        out_vectors.append(flat[place : place + vector.shape[1]])
        place += vector.shape[1]
    gain_one, shift_one, b_query, b_value, b_out, gain_two, shift_two, b_down, b_up = out_vectors
    return (
        gain_one,
        shift_one,
        parts[0],
        b_query,
        parts[1],
        parts[2],
        b_value,
        parts[3],
        b_out,
        gain_two,
        shift_two,
        jnp.concatenate(parts[4:], axis=1),
        b_up,
        down,
        b_down,
    )


def on_device(
    tokens,
    segments,
    ln1_gain,
    ln1_bias,
    w_query,
    b_query,
    w_key,
    w_value,
    b_value,
    w_out,
    b_out,
    ln2_gain,
    ln2_bias,
    w_up,
    b_up,
    w_down,
    b_down,
    out_grad,
):
    layer_count = w_query.shape[0]
    seg_all = lax.all_gather(segments[0].astype(jnp.bfloat16), "ctx", axis=0, tiled=True)
    seg_all = seg_all.astype(jnp.float32)
    place = jnp.arange(seg_all.shape[0])
    allowed = (place[None, :] <= place[:, None]) & (seg_all[None, :] == seg_all[:, None])
    matrices = (w_query, w_key, w_value, w_out, w_up, w_down)
    vectors = (ln1_gain, ln1_bias, b_query, b_value, b_out, ln2_gain, ln2_bias, b_down, b_up)
    every_layer = [
        gather_layer([m[l] for m in matrices], [v[l] for v in vectors])
        for l in range(layer_count)
    ]
    stream = tokens[0].astype(jnp.float32)
    kept_acts = []
    for layer_no in range(layer_count):
        stream, saved_acts = layer_forward(stream, allowed, every_layer[layer_no])
        kept_acts.append(saved_acts)
    output = stream.astype(jnp.bfloat16)[None]
    grad_stream = out_grad[0].astype(jnp.float32)
    collected = [None] * layer_count
    for layer_no in reversed(range(layer_count)):
        grad_stream, terms = layer_back(
            grad_stream, allowed, every_layer[layer_no], kept_acts[layer_no]
        )
        collected[layer_no] = scatter_layer(terms)
    stacked = tuple(jnp.stack(members) for members in zip(*collected))
    return (output, grad_stream[None]) + stacked


def solution(mesh):
    in_specs = (
        P("dp", "ctx", None),
        P("dp", "ctx"),
        P(None, ("dp", "ctx")),
        P(None, ("dp", "ctx")),
        P(None, ("dp", "ctx"), None),
        P(None, ("dp", "ctx")),
        P(None, ("dp", "ctx"), None),
        P(None, ("dp", "ctx"), None),
        P(None, ("dp", "ctx")),
        P(None, ("dp", "ctx"), None),
        P(None, ("dp", "ctx")),
        P(None, ("dp", "ctx")),
        P(None, ("dp", "ctx")),
        P(None, ("dp", "ctx"), None),
        P(None, ("dp", "ctx")),
        P(None, ("dp", "ctx"), None),
        P(None, ("dp", "ctx")),
        P("dp", "ctx", None),
    )
    out_specs = (
        P("dp", "ctx", None),
        P("dp", "ctx", None),
        P(None, ("dp", "ctx")),
        P(None, ("dp", "ctx")),
        P(None, ("dp", "ctx"), None),
        P(None, ("dp", "ctx")),
        P(None, ("dp", "ctx"), None),
        P(None, ("dp", "ctx"), None),
        P(None, ("dp", "ctx")),
        P(None, ("dp", "ctx"), None),
        P(None, ("dp", "ctx")),
        P(None, ("dp", "ctx")),
        P(None, ("dp", "ctx")),
        P(None, ("dp", "ctx"), None),
        P(None, ("dp", "ctx")),
        P(None, ("dp", "ctx"), None),
        P(None, ("dp", "ctx")),
    )
    return jax.shard_map(
        on_device, mesh=mesh, in_specs=in_specs, out_specs=out_specs, check_vma=False
    )
```

```python
import jax
import jax.numpy as jnp
from jax import lax
from jax.sharding import PartitionSpec as P

H = 12
HD = 64


EPSILON = 1e-05
MASKED = -1e30


def matmul(left_op, right_op):
    return jnp.dot(left_op, right_op, preferred_element_type=jnp.float32)


def contract_rows(left_op, right_op):
    return lax.dot_general(
        left_op, right_op, (((0,), (0,)), ((), ())), preferred_element_type=jnp.float32
    )


def contract_cols(left_op, right_op):
    return lax.dot_general(
        left_op, right_op, (((1,), (1,)), ((), ())), preferred_element_type=jnp.float32
    )


def normalize(values):
    centre = jnp.mean(values, axis=-1, keepdims=True)
    centred = values - centre
    scale_vec = lax.rsqrt(jnp.mean(centred * centred, axis=-1, keepdims=True) + EPSILON)
    return (centred * scale_vec, scale_vec)


def norm_back(grad_in, normed, scale_vec, gain_vec):
    scaled = grad_in * gain_vec
    return scale_vec * (
        scaled
        - jnp.mean(scaled, axis=-1, keepdims=True)
        - normed * jnp.mean(scaled * normed, axis=-1, keepdims=True)
    )


def to_heads(blocks_in, parts):
    shards = lax.axis_size("ctx")
    row_count = blocks_in[0].shape[0]
    per = -(-H // shards)
    spare = (per * shards - H) * HD
    sent = jnp.stack([jnp.pad(b, ((0, 0), (0, spare))) for b in blocks_in])
    sent = sent.reshape(parts, row_count, shards, per * HD).transpose(2, 0, 1, 3)
    got = lax.all_to_all(sent, "ctx", 0, 0, tiled=True)
    got = got.reshape(shards, parts, row_count, per, HD).transpose(1, 3, 0, 2, 4)
    return got.reshape(parts, per, shards * row_count, HD)


def from_heads(heads_in):
    shards = lax.axis_size("ctx")
    parts, per, seq_len = heads_in.shape[:3]
    row_count = seq_len // shards
    sent = heads_in.reshape(parts, per, shards, row_count, HD).transpose(2, 0, 3, 1, 4)
    sent = sent.reshape(shards, parts, row_count, per * HD)
    got = lax.all_to_all(sent, "ctx", 0, 0, tiled=True)
    got = got.transpose(1, 2, 0, 3).reshape(parts, row_count, shards * per * HD)
    return got[:, :, : H * HD]


def head_dot(left_op, right_op, left_dim, right_dim):
    return lax.dot_general(
        left_op,
        right_op,
        (((left_dim,), (right_dim,)), ((0,), (0,))),
        preferred_element_type=jnp.float32,
    )


def attend_forward(heads, allowed):
    queries, key_rows, values = heads[0], heads[1], heads[2]
    scores = head_dot(queries, key_rows, 2, 2) * HD ** (-0.5)
    scores = jnp.where(allowed[None], scores, MASKED)
    highest = jnp.max(scores, axis=-1, keepdims=True)
    weights = jnp.exp(scores - highest)
    totals = jnp.sum(weights, axis=-1, keepdims=True)
    mixed_out = head_dot(weights.astype(jnp.bfloat16), values, 2, 1) / totals
    return (mixed_out, highest + jnp.log(totals))


def attend_back(heads, mixed_out, grad_mixed, log_total, allowed):
    queries, key_rows, values = heads[0], heads[1], heads[2]
    score_scale = HD ** (-0.5)
    row_delta = jnp.sum(grad_mixed.astype(jnp.float32) * mixed_out, axis=-1, keepdims=True)
    scores = head_dot(queries, key_rows, 2, 2) * score_scale
    probs = jnp.exp(jnp.where(allowed[None], scores, MASKED) - log_total)
    grad_p = head_dot(grad_mixed, values, 2, 2)
    grad_s = (probs * (grad_p - row_delta)).astype(jnp.bfloat16)
    grad_q = head_dot(grad_s, key_rows, 2, 1) * score_scale
    grad_k = head_dot(grad_s, queries, 1, 1) * score_scale
    grad_v = head_dot(probs.astype(jnp.bfloat16), grad_mixed, 1, 1)
    return jnp.stack([grad_q, grad_k, grad_v]).astype(jnp.bfloat16)


def layer_forward(stream, allowed, gathered):
    w_qkv, w_out, w_up, w_down, vectors = gathered
    gain_one, shift_one, b_query, b_value, b_out, gain_two, shift_two, b_down, b_up = vectors
    width = w_out.shape[1]
    normed_one, scale_one = normalize(stream)
    inputs_one = (normed_one * gain_one + shift_one).astype(jnp.bfloat16)
    bias_all = jnp.concatenate([b_query, jnp.zeros_like(b_query), b_value])
    projected = (matmul(inputs_one, w_qkv) + bias_all).astype(jnp.bfloat16)
    heads = to_heads([projected[:, p * width : (p + 1) * width] for p in range(3)], 3)
    mixed_out, log_total = attend_forward(heads, allowed)
    mixed_low = from_heads(mixed_out.astype(jnp.bfloat16)[None])[0]
    stream_mid = stream + matmul(mixed_low, w_out) + b_out
    normed_two, scale_two = normalize(stream_mid)
    inputs_two = (normed_two * gain_two + shift_two).astype(jnp.bfloat16)
    hidden = matmul(inputs_two, w_up) + b_up
    active = jax.nn.gelu(hidden, approximate=True).astype(jnp.bfloat16)
    stream_out = stream_mid + matmul(active, w_down) + b_down
    saved_acts = (
        normed_one,
        scale_one,
        inputs_one,
        heads,
        mixed_out,
        log_total,
        mixed_low,
        normed_two,
        scale_two,
        inputs_two,
        hidden,
        active,
    )
    return (stream_out, saved_acts)


def column_sums(values):
    return jnp.sum(values, axis=0, dtype=jnp.float32)


def layer_back(grad_out, allowed, gathered, saved_acts):
    w_qkv, w_out, w_up, w_down, vectors = gathered
    gain_one, shift_one, b_query, b_value, b_out, gain_two, shift_two, b_down, b_up = vectors
    (
        normed_one,
        scale_one,
        inputs_one,
        heads,
        mixed_out,
        log_total,
        mixed_low,
        normed_two,
        scale_two,
        inputs_two,
        hidden,
        active,
    ) = saved_acts
    width = w_out.shape[1]
    grad_branch = grad_out.astype(jnp.bfloat16)
    g_b_down = column_sums(grad_branch)
    g_w_down = contract_rows(active, grad_branch)
    grad_active = contract_cols(grad_branch, w_down)
    gelu_value, gelu_pull = jax.vjp(
        lambda inner_val: jax.nn.gelu(inner_val, approximate=True), hidden
    )
    grad_hidden = gelu_pull(grad_active)[0].astype(jnp.bfloat16)
    g_b_up = column_sums(grad_hidden)
    g_w_up = contract_rows(inputs_two, grad_hidden)
    grad_in_two = contract_cols(grad_hidden, w_up)
    g_gain_two = jnp.sum(grad_in_two * normed_two, axis=0)
    g_shift_two = jnp.sum(grad_in_two, axis=0)
    grad_mid = grad_out + norm_back(grad_in_two, normed_two, scale_two, gain_two)
    grad_attn = grad_mid.astype(jnp.bfloat16)
    g_b_out = column_sums(grad_attn)
    g_w_out = contract_rows(mixed_low, grad_attn)
    grad_mixed = contract_cols(grad_attn, w_out).astype(jnp.bfloat16)
    grad_heads = attend_back(
        heads, mixed_out, to_heads([grad_mixed], 1)[0], log_total, allowed
    )
    back = from_heads(grad_heads)
    projected = jnp.concatenate([back[0], back[1], back[2]], axis=1)
    g_bias = column_sums(projected)
    g_proj = contract_rows(inputs_one, projected)
    grad_in_one = contract_cols(projected, w_qkv)
    g_gain_one = jnp.sum(grad_in_one * normed_one, axis=0)
    g_shift_one = jnp.sum(grad_in_one, axis=0)
    grad_stream = grad_mid + norm_back(grad_in_one, normed_one, scale_one, gain_one)
    g_vectors = (
        g_gain_one,
        g_shift_one,
        g_bias[:width],
        g_bias[2 * width :],
        g_b_out,
        g_gain_two,
        g_shift_two,
        g_b_down,
        g_b_up,
    )
    return (grad_stream, (g_proj, g_w_out, g_w_up, g_w_down, g_vectors))


def column_pieces(matrix, width):
    return [matrix[..., c : c + width] for c in range(0, matrix.shape[-1], width)]


def pack_vectors(vectors, width, rows_before):
    joined = jnp.concatenate(vectors, axis=-1)
    short = -joined.shape[-1] % width
    rows = (joined.shape[-1] + short) // width
    short += width * (-(rows_before + rows) % 16)
    joined = jnp.pad(joined, ((0, 0),) * (joined.ndim - 1) + ((0, short),))
    return joined.reshape(joined.shape[:-1] + (-1, width))


def gather_layer(matrices, vectors):
    w_query, w_key, w_value, w_out, w_up, w_down = matrices
    width = w_query.shape[1]
    pieces = [w_query, w_key, w_value, w_out] + column_pieces(w_up, width) + [w_down]
    pieces.append(pack_vectors(vectors, width, sum(p.shape[0] for p in pieces)))
    packed = jnp.concatenate(pieces, axis=0)
    return lax.all_gather(packed, ("dp", "ctx"), axis=0, tiled=False)


def unpack_layer(whole, matrices, vectors):
    w_query, w_key, w_value, w_out, w_up, w_down = matrices
    rows, width = w_query.shape
    up_count = w_up.shape[1] // width

    def taken(first, count):
        return whole[:, first : first + count].reshape(-1, width)

    parts = [taken(i * rows, rows) for i in range(4 + up_count)]
    start = (4 + up_count) * rows
    down = taken(start, w_down.shape[0])
    start += w_down.shape[0]
    flat = whole[:, start:].reshape(whole.shape[0], -1)
    out_vectors = []
    place = 0
    for vector in vectors:
        out_vectors.append(flat[:, place : place + vector.shape[0]].reshape(-1))
        place += vector.shape[0]
    return (
        jnp.concatenate(parts[:3], axis=1),
        parts[3],
        jnp.concatenate(parts[4:], axis=1),
        down,
        tuple(out_vectors),
    )


def scatter_terms(blocks, vectors):
    width = blocks[0].shape[1]
    shards = lax.axis_size(("dp", "ctx"))
    blocks = [b.astype(jnp.bfloat16).reshape(shards, -1, width) for b in blocks]
    vectors = [v.astype(jnp.bfloat16).reshape(shards, -1) for v in vectors]
    last = pack_vectors(vectors, width, sum(b.shape[1] for b in blocks))
    own = lax.psum_scatter(
        jnp.concatenate(blocks + [last], axis=1),
        ("dp", "ctx"),
        scatter_dimension=0,
        tiled=False,
    ).astype(jnp.float32)
    out_blocks, out_vectors = [], []
    start = 0
    for block in blocks:
        out_blocks.append(own[start : start + block.shape[1]])
        start += block.shape[1]
    flat = own[start:].reshape(-1)
    place = 0
    for vector in vectors:
        out_vectors.append(flat[place : place + vector.shape[1]])
        place += vector.shape[1]
    return out_blocks, out_vectors


def scatter_all(collected):
    early, late = [], []
    for layer_no in reversed(range(len(collected))):
        g_proj, g_w_out, g_w_up, g_w_down, g_vectors = collected[layer_no]
        width = g_w_out.shape[1]
        feed = (layer_no, 0, [g_w_out] + column_pieces(g_w_up, width) + [g_w_down], g_vectors[4:])
        attn = (layer_no, 1, column_pieces(g_proj, width), g_vectors[:4])
        (late if early else early).append(feed)
        late.append(attn)
    found = {}
    for group in (early, late):
        blocks, vectors = scatter_terms(
            [b for entry in group for b in entry[2]], [v for entry in group for v in entry[3]]
        )
        for layer_no, kind, in_blocks, in_vectors in group:
            found[layer_no, kind] = (blocks[: len(in_blocks)], vectors[: len(in_vectors)])
            blocks, vectors = blocks[len(in_blocks) :], vectors[len(in_vectors) :]
    results = []
    for layer_no in range(len(collected)):
        feed, feed_vectors = found[layer_no, 0]
        proj, proj_vectors = found[layer_no, 1]
        gain_one, shift_one, b_query, b_value = proj_vectors
        b_out, gain_two, shift_two, b_down, b_up = feed_vectors
        up = jnp.concatenate(feed[1:-1], axis=1)
        results.append(
            (gain_one, shift_one, proj[0], b_query, proj[1], proj[2], b_value)
            + (feed[0], b_out, gain_two, shift_two, up, b_up, feed[-1], b_down)
        )
    return results


def on_device(
    tokens,
    segments,
    ln1_gain,
    ln1_bias,
    w_query,
    b_query,
    w_key,
    w_value,
    b_value,
    w_out,
    b_out,
    ln2_gain,
    ln2_bias,
    w_up,
    b_up,
    w_down,
    b_down,
    out_grad,
):
    layer_count = w_query.shape[0]
    seg_all = lax.all_gather(segments[0].astype(jnp.bfloat16), "ctx", axis=0, tiled=True)
    seg_all = seg_all.astype(jnp.float32)
    place = jnp.arange(seg_all.shape[0])
    allowed = (place[None, :] <= place[:, None]) & (seg_all[None, :] == seg_all[:, None])
    matrices = (w_query, w_key, w_value, w_out, w_up, w_down)
    vectors = (ln1_gain, ln1_bias, b_query, b_value, b_out, ln2_gain, ln2_bias, b_down, b_up)
    shards = [([m[l] for m in matrices], [v[l] for v in vectors]) for l in range(layer_count)]
    packed = [gather_layer(*own) for own in shards]
    every_layer = []
    stream = tokens[0].astype(jnp.float32)
    kept_acts = []
    for layer_no in range(layer_count):
        whole = packed[layer_no]
        if layer_no > 0:
            stream, whole = lax.optimization_barrier((stream, whole))
        every_layer.append(unpack_layer(whole, *shards[layer_no]))
        stream, saved_acts = layer_forward(stream, allowed, every_layer[layer_no])
        kept_acts.append(saved_acts)
    output = stream.astype(jnp.bfloat16)[None]
    grad_stream = out_grad[0].astype(jnp.float32)
    collected = [None] * layer_count
    for layer_no in reversed(range(layer_count)):
        grad_stream, terms = layer_back(
            grad_stream, allowed, every_layer[layer_no], kept_acts[layer_no]
        )
        collected[layer_no] = terms
    stacked = tuple(jnp.stack(members) for members in zip(*scatter_all(collected)))
    return (output, grad_stream[None]) + stacked


def solution(mesh):
    in_specs = (
        P("dp", "ctx", None),
        P("dp", "ctx"),
        P(None, ("dp", "ctx")),
        P(None, ("dp", "ctx")),
        P(None, ("dp", "ctx"), None),
        P(None, ("dp", "ctx")),
        P(None, ("dp", "ctx"), None),
        P(None, ("dp", "ctx"), None),
        P(None, ("dp", "ctx")),
        P(None, ("dp", "ctx"), None),
        P(None, ("dp", "ctx")),
        P(None, ("dp", "ctx")),
        P(None, ("dp", "ctx")),
        P(None, ("dp", "ctx"), None),
        P(None, ("dp", "ctx")),
        P(None, ("dp", "ctx"), None),
        P(None, ("dp", "ctx")),
        P("dp", "ctx", None),
    )
    out_specs = (
        P("dp", "ctx", None),
        P("dp", "ctx", None),
        P(None, ("dp", "ctx")),
        P(None, ("dp", "ctx")),
        P(None, ("dp", "ctx"), None),
        P(None, ("dp", "ctx")),
        P(None, ("dp", "ctx"), None),
        P(None, ("dp", "ctx"), None),
        P(None, ("dp", "ctx")),
        P(None, ("dp", "ctx"), None),
        P(None, ("dp", "ctx")),
        P(None, ("dp", "ctx")),
        P(None, ("dp", "ctx")),
        P(None, ("dp", "ctx"), None),
        P(None, ("dp", "ctx")),
        P(None, ("dp", "ctx"), None),
        P(None, ("dp", "ctx")),
    )
    return jax.shard_map(
        on_device, mesh=mesh, in_specs=in_specs, out_specs=out_specs, check_vma=False
    )
```
